1024 devices in a mesh: expert: 64 (over y, z_hi, core), tensor: 16 (over z_lo, x).
Axes of the slice: x: 8, y: 8, z: 8 (z_hi: 4, z_lo: 2; z = z_hi * 2 + z_lo), core: 2. Of those that a mesh axis runs over, the one named last changes fastest.
Arguments:
- tokens: bfloat16 [4096, 4096], P('expert', 'tensor'), may hold values from -6 to 6
- expert_ids: int32 [4096, 8], P('expert'), may hold values from 0 to 63, all different within a row; in each aligned block of 64 rows (0 to 63, 64 to 127, ...) at most 12 rows name the same one
- gate_weights: float32 [4096, 8], P('expert'), may hold values from 0.1 to 1
- w_gate: bfloat16 [64, 4096, 1536], P('expert', None, 'tensor'), may hold values from -0.09375 to 0.09375
- w_up: bfloat16 [64, 4096, 1536], P('expert', None, 'tensor'), may hold values from -0.09375 to 0.09375
- w_down: bfloat16 [64, 1536, 4096], P('expert', 'tensor'), may hold values from -0.15625 to 0.15625
Outputs:
- mixed: bfloat16 [4096, 4096], P('expert', 'tensor')
The draws below stay inside these ranges and needn't reach their ends.
Inputs may be any that keep to these rules, and one draw needn't show every extreme that they name: `expert_ids`: each row names 8 different experts. Within each aligned block of 64 rows no expert is named by more than 12 rows, and in every draw some expert is named by exactly 12 rows of some block.
All inputs are finite; a program needn't handle non-finite values.
Results may differ from the reference program's by a relative error of at most 0.02.
Values may be sent and summed in bfloat16 or wider, within the bound.
A program may use at most 64 MiB of HBM per device.

```python
import math
import jax
import jax.numpy as jnp
import numpy as np
from jax import lax

D = 4096
FF = 1536
TOP = 8
TOK_DEV = 64
EXPERTS = 64
CAP = 12
TOKENS = 4096
N_EXPERT = 64
N_TENSOR = 16


def level_of(rng, shape, shards, low, high):
    gain, own = 1.0, jax.random.fold_in(rng, 6)
    for dim, shards_of in shards:
        draws = jnp.exp(jax.random.uniform(jax.random.fold_in(own, dim), (shards_of,), jnp.float32, low / len(shards), high / len(shards)))
        gain = gain * jnp.repeat(draws, shape[dim] // shards_of).reshape([-1 if axis == dim else 1 for axis in range(len(shape))])
    return gain


def shared_out(rng, own, number, rows, count, top, reach, skew):
    order = jax.random.permutation(rng, count)
    heavy_load, common = load_shares(count, rows * top, reach, skew, True), load_shares(count, rows * top, reach, skew, False)
    places = jnp.arange(count)

    def named(tallies, offset_by):
        used = int((tallies > 0).sum())
        fixed = max(1, used // 4)
        shifted = fixed + (places - fixed + offset_by * (used - fixed)) % max(1, count - fixed)
        return jnp.zeros((count,), jnp.int32).at[order[jnp.where(places < fixed, places, shifted)]].set(jnp.asarray(tallies, jnp.int32))

    tallies = jnp.where(number % 4 == 0, named(heavy_load, number // 4), named(common, number - number // 4 - 1))
    mixed = jax.random.permutation(jax.random.fold_in(own, 3), count)
    giver, sink = mixed[0:count // 2 * 2:2], mixed[1:count // 2 * 2:2]
    margin = jnp.minimum(tallies[giver] - 1, reach - tallies[sink]) // 2
    margin = jnp.where((giver == order[0]) | (sink == order[0]) | (tallies[sink] == 0), 0, jnp.maximum(margin, 0))
    shifted = jax.random.randint(jax.random.fold_in(own, 4), (count // 2,), 0, 1 << 20) % (margin + 1)
    tallies = tallies.at[giver].add(-shifted).at[sink].add(shifted)
    labels = jnp.searchsorted(jnp.cumsum(tallies), jnp.arange(rows * top), side="right").astype(jnp.int32)
    listing = labels.reshape(top, rows).T
    listing = listing[jax.random.permutation(jax.random.fold_in(own, 1), rows)]
    offset_by = jax.random.randint(jax.random.fold_in(own, 2), (rows, 1), 0, top)
    return jnp.take_along_axis(listing, (jnp.arange(top)[None, :] + offset_by) % top, axis=1)


def load_shares(amount, total, reach, skew, full):
    portions = [(1 << 20) // math.isqrt(grade ** skew) + 1 for grade in range(1, amount + 1)]
    largest = reach if full else min(reach, max(-(-total // amount), total * portions[0] // sum(portions)))
    least = 1 if total - largest >= amount - 1 else 0
    counts, rest = [largest] + [least] * (amount - 1), total - largest - least * (amount - 1)
    while rest > 0:
        free = [i for i in range(1, amount) if counts[i] < largest] or [i for i in range(1, amount) if counts[i] < reach]
        pool, remaining = sum([portions[i] for i in free]), rest
        for i in free:
            extra = min(reach - counts[i], max(1, remaining * portions[i] // pool), rest)
            counts[i] = counts[i] + extra
            rest = rest - extra
    return np.array(counts)


def bell_draw(own_key, shape, scale, bound, shards=(), held_as=jnp.bfloat16):
    array = jax.random.normal(own_key, shape, jnp.float32) * scale
    if len(shards) > 0:
        array = level_of(own_key, shape, shards, -0.22, 0.18) * array
    return jnp.clip(array, min=-bound, max=bound).astype(held_as)


def setup_inputs(seed: int = 0) -> dict:
    key_of = jax.random.split(jax.random.key(seed), 7)
    tokens = bell_draw(key_of[0], (TOKENS, D), 1.0, 6.0, ((0, 64), (1, 16)))
    expert_ids_keys = jax.random.split(jax.random.fold_in(key_of[1], 1), TOKENS // TOK_DEV)
    expert_ids_turns = jax.random.permutation(jax.random.fold_in(key_of[1], 3), TOKENS // TOK_DEV)
    expert_ids = jax.vmap(lambda own, number: shared_out(jax.random.fold_in(key_of[1], 2), own, number, TOK_DEV, EXPERTS, TOP, CAP, 2))(expert_ids_keys, expert_ids_turns).reshape((TOKENS, TOP))
    gate_weights = jnp.clip(0.1 + 0.9 * jax.random.uniform(key_of[2], (TOKENS, TOP), jnp.float32) ** level_of(key_of[2], (TOKENS, TOP), ((0, 64),), -0.2, 0.2), 0.1, 1.0)
    w_gate = bell_draw(key_of[3], (EXPERTS, D, FF), D ** -0.5, 0.09375, ((0, 64), (2, 16)))
    w_up = bell_draw(key_of[4], (EXPERTS, D, FF), D ** -0.5, 0.09375, ((0, 64), (2, 16)))
    w_down = bell_draw(key_of[5], (EXPERTS, FF, D), FF ** -0.5, 0.15625, ((0, 64), (1, 16)))
    return dict(tokens=tokens, expert_ids=expert_ids, gate_weights=gate_weights, w_gate=w_gate, w_up=w_up, w_down=w_down)


def run_expert(operands):
    rows_in, gate_mat, up_mat, down_mat = operands
    gate = jnp.dot(rows_in, gate_mat, preferred_element_type=jnp.float32)
    up_val = jnp.dot(rows_in, up_mat, preferred_element_type=jnp.float32)
    hidden = (jax.nn.silu(gate) * up_val).astype(jnp.bfloat16)
    shard = FF // N_TENSOR
    hidden_blocks = hidden.reshape(hidden.shape[0], N_TENSOR, shard).astype(jnp.float32)
    down_blocks = down_mat.reshape(N_TENSOR, shard, D).astype(jnp.float32)
    partial_value = jnp.einsum("rsf,sfd->srd", hidden_blocks, down_blocks)
    rounded = lax.optimization_barrier(partial_value.astype(jnp.bfloat16))
    return jnp.sum(rounded.astype(jnp.float32), axis=0).astype(jnp.bfloat16)


def reference(tokens, expert_ids, gate_weights, w_gate, w_up, w_down):
    blocks = expert_ids.reshape(N_EXPERT, TOK_DEV * TOP)
    expert_range = jnp.arange(EXPERTS).astype(jnp.int32)
    onehot = (blocks[:, :, None] == expert_range[None, None, :]).astype(jnp.int32)
    slot_rank = jnp.sum((jnp.cumsum(onehot, axis=1) - onehot) * onehot, axis=2).astype(jnp.int32)
    block_index = jnp.arange(N_EXPERT).astype(jnp.int32)[:, None]
    slot_row = (block_index * CAP + slot_rank).astype(jnp.int32)
    flat_experts = blocks.reshape(-1)
    flat_rows = slot_row.reshape(-1)
    token_index = (jnp.arange(TOKENS * TOP) // TOP).astype(jnp.int32)
    dispatched = jnp.zeros((EXPERTS, N_EXPERT * CAP, D), jnp.bfloat16)
    dispatched = dispatched.at[flat_experts, flat_rows].set(tokens[token_index])
    expert_out = lax.map(run_expert, (dispatched, w_gate, w_up, w_down))
    picked = expert_out[flat_experts, flat_rows].reshape(TOKENS, TOP, D)
    mixed = jnp.sum(gate_weights[:, :, None] * picked.astype(jnp.float32), axis=1)
    return mixed.astype(jnp.bfloat16)
```

```python
import functools

import jax
import jax.numpy as jnp
from jax import lax
from jax.experimental import pallas as pl
from jax.experimental.pallas import tpu as pltpu
from jax.sharding import PartitionSpec as P

MESH = pl.DeviceIdType.MESH
BF16, F32, I32 = jnp.bfloat16, jnp.float32, jnp.int32
CAP = 12
PAD = 16
CHUNKS = 2


def nt(a, b):
    return lax.dot_general(a, b, (((1,), (1,)), ((), ())), preferred_element_type=F32)


def nn(a, b):
    return jnp.dot(a, b, preferred_element_type=F32)


def tn(a, b):
    return lax.dot_general(a, b, (((0,), (0,)), ((), ())), preferred_element_type=F32)


def iota(shape, dim):
    return lax.broadcasted_iota(I32, shape, dim)


def kernel(
    E, NX,
    tok_ref, ids_ref, gw_ref, wg_ref, wu_ref, wd_ref, out_ref,
    send_buf, recv_buf, xa, xb, w1, acc, hid, wdn, out_acc, ret_src, ret_buf, comb,
    sem_w, sem_disp, sem_w1, sem_wds, sem_wdr, sem_fwd, sem_xs, sem_xr, sem_hs, sem_hr, sem_ret,
):
    HALF = E // 2
    TOK, F = tok_ref.shape
    U = wg_ref.shape[0]
    ROWS = HALF * CAP
    RC = ROWS // CHUNKS
    me = lax.axis_index("expert")
    s = lax.axis_index("tensor")
    z, x = s // NX, s % NX
    right, left = (x + 1) % NX, (x + NX - 1) % NX
    other = 1 - z
    home = me % 2
    own = home == z

    barrier = pltpu.get_barrier_semaphore()

    def greet(i, _):
        for zz in range(2):
            @pl.when(jnp.logical_not(jnp.logical_and(2 * i + z == me, zz == z)))
            def _():
                pl.semaphore_signal(barrier, inc=1, device_id=(2 * i + z, zz * NX + x), device_id_type=MESH)
        return 0

    lax.fori_loop(0, HALF, greet, 0)

    def greet_x(d, _):
        pl.semaphore_signal(barrier, inc=1, device_id=(me, z * NX + (x + d) % NX), device_id_type=MESH)
        return 0

    lax.fori_loop(1, NX, greet_x, 0)
    pl.semaphore_signal(barrier, inc=1, device_id=(me, other * NX + x), device_id_type=MESH)

    def cols(zz, xx):
        return pl.ds(pl.multiple_of(zz * (NX * F) + xx * F, F), F)

    def units(xx, zz):
        return pl.ds(pl.multiple_of((xx * 2 + zz) * U, U), U)

    load_g = pltpu.make_async_copy(wg_ref, w1.at[z, 0:U], sem_w.at[0])
    load_u = pltpu.make_async_copy(wu_ref, w1.at[z, U:2 * U], sem_w.at[1])
    load_d = [
        pltpu.make_async_copy(wd_ref.at[:, cols(f, x)], wdn.at[f, units(x, z)], sem_w.at[2 + f])
        for f in range(2)
    ]
    for c in (load_g, load_u, *load_d):
        c.start()

    ids = ids_ref[...]
    expert = iota((E, TOK), 0)
    member = jnp.zeros((E, TOK), jnp.bool_)
    weight = jnp.zeros((E, TOK), F32)
    for k in range(ids.shape[0]):
        hit = ids[k:k + 1, :] == expert
        member = jnp.logical_or(member, hit)
        weight = weight + jnp.where(hit, gw_ref[k:k + 1, :], 0.0)
    before = (iota((TOK, TOK), 0) < iota((TOK, TOK), 1)).astype(BF16)
    rank = nn(member.astype(F32).astype(BF16), before).astype(I32)
    rank = jnp.where(member, rank, PAD)
    slot = iota((E, PAD, TOK), 1)
    chosen = slot == rank[:, None, :]
    select = jnp.where(chosen, 1.0, 0.0).reshape(E * PAD, TOK).astype(BF16)
    send_buf[...] = nn(select, tok_ref[...]).astype(BF16).reshape(E, PAD, F)
    weights = jnp.where(chosen, weight[:, None, :], 0.0).reshape(E * PAD, TOK)
    high = weights.astype(BF16)
    comb[0] = high
    comb[1] = (weights - high.astype(F32)).astype(BF16)

    @pl.when(own)
    def _():
        pl.semaphore_wait(barrier, NX + E - 1)

    @pl.when(jnp.logical_not(own))
    def _():
        pl.semaphore_wait(barrier, NX + E)

    def dispatch(e, _):
        here = jnp.logical_and(e == me, own)

        @pl.when(here)
        def _():
            pltpu.make_async_copy(send_buf.at[e], recv_buf.at[z, me // 2], sem_disp.at[1]).start()

        @pl.when(jnp.logical_not(here))
        def _():
            pltpu.make_async_remote_copy(
                src_ref=send_buf.at[e], dst_ref=recv_buf.at[z, me // 2],
                send_sem=sem_disp.at[0], recv_sem=sem_disp.at[1],
                device_id=(e, home * NX + x), device_id_type=MESH,
            ).start()
        return 0

    lax.fori_loop(0, E, dispatch, 0)

    pair = (me, other * NX + x)
    send_w1 = [
        pltpu.make_async_remote_copy(
            src_ref=src, dst_ref=w1.at[z, j * U:(j + 1) * U],
            send_sem=sem_w1.at[0, j], recv_sem=sem_w1.at[1, j], device_id=pair, device_id_type=MESH,
        )
        for j, src in enumerate((wg_ref, wu_ref))
    ]
    for c in send_w1:
        c.start()

    def down(d, f):
        to = (x + d) % NX
        return pltpu.make_async_remote_copy(
            src_ref=wd_ref.at[:, cols(f, to)], dst_ref=wdn.at[f, units(x, z)],
            send_sem=sem_wds.at[d, f], recv_sem=sem_wdr.at[d, f],
            device_id=(me, z * NX + to), device_id_type=MESH,
        )

    def down_start(d, _):
        for f in range(2):
            down(d, f).start()
        return 0

    lax.fori_loop(1, NX, down_start, 0)

    def relay(d, f):
        part = wdn.at[f, units((x - d + NX) % NX, z)]
        return pltpu.make_async_remote_copy(
            src_ref=part, dst_ref=part, send_sem=sem_fwd.at[0, d, f], recv_sem=sem_fwd.at[1, d, f],
            device_id=pair, device_id_type=MESH,
        )

    everything = pltpu.make_async_copy(send_buf, send_buf, sem_disp.at[1])
    everything.wait()
    row, col = iota((ROWS, HALF * PAD), 0), iota((ROWS, HALF * PAD), 1)
    place = (col >> 4) * CAP + (col & 15)
    pack = jnp.logical_and(row == place, (col & 15) < CAP)
    pack = jnp.where(pack, 1.0, 0.0).astype(BF16)
    xa[x] = nn(pack, recv_buf[0].reshape(HALF * PAD, F)).astype(BF16)
    xb[x] = nn(pack, recv_buf[1].reshape(HALF * PAD, F)).astype(BF16)

    def ring(k, c, way):
        buf, shard, to = ((xa, (x - k + NX) % NX, right), (xb, (x + k) % NX, left))[way]
        part = buf.at[shard, pl.ds(c * RC, RC)]
        return pltpu.make_async_remote_copy(
            src_ref=part, dst_ref=part, send_sem=sem_xs.at[k, c, way], recv_sem=sem_xr.at[k, c, way],
            device_id=(me, z * NX + to), device_id_type=MESH,
        )

    def multiply(zz, k):
        a, b = (x - k + NX) % NX, (x + k) % NX
        acc[zz] += nt(w1[zz, :, cols(0, a)], xa[a]) + nt(w1[zz, :, cols(1, b)], xb[b])

    for c in range(CHUNKS):
        for way in range(2):
            ring(0, c, way).start()
    for c in (load_g, load_u, *load_d):
        c.wait()
    acc[...] = jnp.zeros_like(acc)
    multiply(z, 0)
    for f in range(2):
        relay(0, f).start()

    def ring_step(k, _):
        for c in range(CHUNKS):
            for way in range(2):
                ring(k - 1, c, way).wait_recv()

                @pl.when(k < NX - 1)
                def _():
                    ring(k, c, way).start()
        multiply(z, k)
        for f in range(2):
            down(k, f).wait_recv()
            relay(k, f).start()
        return 0

    lax.fori_loop(1, NX, ring_step, 0)

    for c in send_w1:
        c.wait_recv()

    def rest(k, _):
        multiply(other, k)
        return 0

    lax.fori_loop(0, NX, rest, 0)

    for zz in range(2):
        g, u = acc[zz, 0:U, :], acc[zz, U:2 * U, :]
        hid[x, zz * U:(zz + 1) * U, :] = (g / (1.0 + jnp.exp(-g)) * u).astype(BF16)

    def hring(k, way):
        shard, to = (((x - k + NX) % NX, right), ((x + k) % NX, left))[way]
        part = hid.at[shard, way * U:(way + 1) * U]
        return pltpu.make_async_remote_copy(
            src_ref=part, dst_ref=part, send_sem=sem_hs.at[k, way], recv_sem=sem_hr.at[k, way],
            device_id=(me, z * NX + to), device_id_type=MESH,
        )

    for way in range(2):
        hring(0, way).start()

    prow, pcol = iota((HALF * PAD, ROWS), 0), iota((HALF * PAD, ROWS), 1)
    spread = jnp.logical_and(pcol == (prow >> 4) * CAP + (prow & 15), (prow & 15) < CAP)
    spread = jnp.where(spread, 1.0, 0.0).astype(BF16)

    def project(k):
        for way in range(2):
            shard = ((x - k + NX) % NX, (x + k) % NX)[way]
            rows = nt(spread, hid[shard, way * U:(way + 1) * U, :]).astype(BF16)
            for f in range(2):
                out_acc[f] += nn(rows, wdn[f, units(shard, way), :])

    def relay_wait(k, _):
        for f in range(2):
            relay(k, f).wait_recv()
        return 0

    lax.fori_loop(0, NX, relay_wait, 0)
    out_acc[...] = jnp.zeros_like(out_acc)
    project(0)

    def hidden_step(k, _):
        for way in range(2):
            hring(k - 1, way).wait_recv()

            @pl.when(k < NX - 1)
            def _():
                hring(k, way).start()
        project(k)
        return 0

    lax.fori_loop(1, NX, hidden_step, 0)
    ret_src[...] = out_acc[...].astype(BF16).reshape(2, HALF, PAD, F)

    def give_back(i, _):
        for f in range(2):
            here = jnp.logical_and(2 * i + z == me, f == z)

            @pl.when(here)
            def _():
                pltpu.make_async_copy(ret_src.at[f, i], ret_buf.at[me], sem_ret.at[1]).start()

            @pl.when(jnp.logical_not(here))
            def _():
                pltpu.make_async_remote_copy(
                    src_ref=ret_src.at[f, i], dst_ref=ret_buf.at[me],
                    send_sem=sem_ret.at[0], recv_sem=sem_ret.at[1],
                    device_id=(2 * i + z, f * NX + x), device_id_type=MESH,
                ).start()
        return 0

    lax.fori_loop(0, HALF, give_back, 0)

    for sem, buf in ((sem_disp.at[0], send_buf), (sem_ret.at[0], ret_buf)):
        @pl.when(own)
        def _():
            pltpu.make_async_copy(buf.at[0:E - 1], buf.at[0:E - 1], sem).wait()

        @pl.when(jnp.logical_not(own))
        def _():
            pltpu.make_async_copy(buf, buf, sem).wait()
    for c in send_w1:
        c.wait_send()

    def sent(k, _):
        for f in range(2):
            relay(k, f).wait_send()

            @pl.when(k > 0)
            def _():
                down(k, f).wait_send()

            @pl.when(k < NX - 1)
            def _():
                for c in range(CHUNKS):
                    ring(k, c, f).wait_send()
                hring(k, f).wait_send()
        return 0

    lax.fori_loop(0, NX, sent, 0)

    pltpu.make_async_copy(ret_buf, ret_buf, sem_ret.at[1]).wait()
    back = ret_buf[...].reshape(E * PAD, F)
    out_ref[...] = (tn(comb[0], back) + tn(comb[1], back)).astype(BF16)


def solution(mesh):
    E, T = mesh.shape["expert"], mesh.shape["tensor"]
    NX = T // 2

    def local(tokens, expert_ids, gate_weights, w_gate, w_up, w_down):
        tok, F = tokens.shape
        U = w_gate.shape[2]
        HALF = E // 2
        ROWS = HALF * CAP
        vmem = pl.BlockSpec(memory_space=pltpu.VMEM)
        hbm = pl.BlockSpec(memory_space=pl.ANY)
        dma = pltpu.SemaphoreType.DMA
        return pl.pallas_call(
            functools.partial(kernel, E, NX),
            out_shape=jax.ShapeDtypeStruct((tok, F), BF16),
            in_specs=[vmem, vmem, vmem, hbm, hbm, hbm],
            out_specs=vmem,
            scratch_shapes=[
                pltpu.VMEM((E, PAD, F), BF16),
                pltpu.VMEM((2, HALF, PAD, F), BF16),
                pltpu.VMEM((NX, ROWS, F), BF16),
                pltpu.VMEM((NX, ROWS, F), BF16),
                pltpu.VMEM((2, 2 * U, T * F), BF16),
                pltpu.VMEM((2, 2 * U, ROWS), F32),
                pltpu.VMEM((NX, 2 * U, ROWS), BF16),
                pltpu.VMEM((2, T * U, F), BF16),
                pltpu.VMEM((2, HALF * PAD, F), F32),
                pltpu.VMEM((2, HALF, PAD, F), BF16),
                pltpu.VMEM((E, PAD, F), BF16),
                pltpu.VMEM((2, E * PAD, tok), BF16),
                dma((4,)),
                dma((2,)),
                dma((2, 2)),
                dma((NX, 2)),
                dma((NX, 2)),
                dma((2, NX, 2)),
                dma((NX, CHUNKS, 2)),
                dma((NX, CHUNKS, 2)),
                dma((NX, 2)),
                dma((NX, 2)),
                dma((2,)),
            ],
            compiler_params=pltpu.CompilerParams(
                collective_id=0, has_side_effects=True, vmem_limit_bytes=48 * 2**20
            ),
        )(
            tokens,
            expert_ids.T,
            gate_weights.T,
            w_gate[0].T,
            w_up[0].T,
            w_down[0],
        )

    placed = (
        P("expert", "tensor"),
        P("expert", None),
        P("expert", None),
        P("expert", None, "tensor"),
        P("expert", None, "tensor"),
        P("expert", "tensor", None),
    )
    return jax.shard_map(
        local, mesh=mesh, in_specs=placed, out_specs=P("expert", "tensor"), check_vma=False
    )
```

```python
import functools

import jax
import jax.numpy as jnp
from jax import lax
from jax.experimental import pallas as pl
from jax.experimental.pallas import tpu as pltpu
from jax.sharding import PartitionSpec as P

MESH = pl.DeviceIdType.MESH
BF16, F32, I32 = jnp.bfloat16, jnp.float32, jnp.int32
CAP = 12
PAD = 16
LAG = 2


def nt(a, b):
    return lax.dot_general(a, b, (((1,), (1,)), ((), ())), preferred_element_type=F32)


def nn(a, b):
    return jnp.dot(a, b, preferred_element_type=F32)


def tn(a, b):
    return lax.dot_general(a, b, (((0,), (0,)), ((), ())), preferred_element_type=F32)


def iota(shape, dim):
    return lax.broadcasted_iota(I32, shape, dim)


def loop(low, high, body):
    def step(k, carry):
        body(k)
        return carry

    lax.fori_loop(low, high, step, 0)


def kernel(
    E, NX,
    tok_ref, ids_ref, gw_ref, wg_ref, wu_ref, wd_ref, out_ref,
    send_buf, recv_buf, xs, w1, acc, hid, wdn, wrel, out_acc, ret_src, ret_buf, comb,
    sem_ds, sem_dr, sem_w1s, sem_w1r, sem_wds, sem_wdr, sem_wfs, sem_wfr, sem_wl,
    sem_xs, sem_xr, sem_hs, sem_hr, sem_rs, sem_rr,
):
    HALF = E // 2
    HB = HALF // 2
    TOK, F = tok_ref.shape
    U = wg_ref.shape[0]
    ROWS = HALF * CAP
    RQ = ROWS // 2
    J = F // 2
    FAR = NX // 2
    me = lax.axis_index("expert")
    s = lax.axis_index("tensor")
    z, x = s // NX, s % NX
    pair, core = me // 2, me % 2
    right, left = (x + 1) % NX, (x + NX - 1) % NX
    other = 1 - z
    work = pair * 2 + z
    home = core == z
    place = (pair % 2) * HB + pair // 2
    across = (me, other * NX + x)
    sibling = (pair * 2 + 1 - core, s)

    def remote(src, dst, send, recv, to):
        return pltpu.make_async_remote_copy(
            src_ref=src, dst_ref=dst, send_sem=send, recv_sem=recv, device_id=to, device_id_type=MESH
        )

    def when(condition, body):
        pl.when(condition)(body)

    away = jnp.logical_not(home)

    barrier = pltpu.get_barrier_semaphore()

    def hello(to):
        pl.semaphore_signal(barrier, inc=1, device_id=to, device_id_type=MESH)

    hello(sibling)
    loop(1, NX, lambda d: hello((me, z * NX + (x + d) % NX)))

    def greet(i):
        for zz in range(2):
            when(
                jnp.logical_not(jnp.logical_and(i == pair, zz == z)),
                lambda: hello((2 * i + core, zz * NX + x)),
            )

    loop(0, HALF, greet)

    ids = ids_ref[...]
    expert = iota((E, TOK), 0)
    member = jnp.zeros((E, TOK), jnp.bool_)
    for k in range(ids.shape[0]):
        member = jnp.logical_or(member, ids[k:k + 1, :] == expert)
    before = (iota((TOK, TOK), 0) < iota((TOK, TOK), 1)).astype(BF16)
    rank = nn(member.astype(F32).astype(BF16), before).astype(I32)
    rank = jnp.where(member, rank, PAD)
    chosen = iota((E, PAD, TOK), 1) == rank[:, None, :]
    select = jnp.where(chosen, 1.0, 0.0).reshape(E * PAD, TOK).astype(BF16)
    send_buf[...] = nn(select, tok_ref[...]).astype(BF16).reshape(E, PAD, F)

    pl.semaphore_wait(barrier, 2 * HALF - 1 + NX)

    def cols(zz, xx):
        return pl.ds(pl.multiple_of(zz * (NX * F) + xx * F, F), F)

    def part(zz, j):
        return w1.at[zz, j * U:(j + 1) * U]

    def w1_own(j, to):
        return remote((wg_ref, wu_ref)[j], part(z, j), sem_w1s.at[0, j], sem_w1r.at[z, j], to)

    def w1_local(j):
        return pltpu.make_async_copy((wg_ref, wu_ref)[j], part(z, j), sem_w1r.at[z, j])

    def w1_pass(j):
        return remote(part(other, j), part(other, j), sem_w1s.at[1, j], sem_w1r.at[other, j], sibling)

    def w1_start():
        for j in range(2):
            when(away, lambda: w1_own(j, across).start())
        for j in range(2):
            when(home, lambda: w1_own(j, sibling).start())
            when(home, lambda: w1_local(j).start())

    def w1_arrived(zz):
        for j in range(2):
            pltpu.make_async_copy(part(zz, j), part(zz, j), sem_w1r.at[zz, j]).wait()

    def units(xx):
        return pl.ds(pl.multiple_of(xx * U, U), U)

    def down(d, f, buf):
        to = (x + d) % NX
        return remote(
            wd_ref.at[:, cols(f, to)], buf.at[f, units(x)], sem_wds.at[d, f], sem_wdr.at[d, f],
            (me, z * NX + to),
        )

    def down_local(f, buf):
        return pltpu.make_async_copy(wd_ref.at[:, cols(f, x)], buf.at[f, units(x)], sem_wl.at[f])

    def down_all(buf, act):
        loop(1, NX, lambda d: [act(down(d, f, buf)) for f in range(2)])

    def down_start(buf):
        for f in range(2):
            down_local(f, buf).start()
        down_all(buf, lambda c: c.start())

    def down_arrived(buf):
        for f in range(2):
            down_local(f, buf).wait()
        down_all(buf, lambda c: c.wait_recv())

    def wd_pass(src, zz, to):
        return remote(src, wdn.at[zz], sem_wfs.at[zz], sem_wfr.at[zz], to)


    def lanes(j):
        return pl.ds(j * J, J)

    def dispatch(j):
        def one(e):
            here = e == work
            src, dst = send_buf.at[e, :, lanes(j)], recv_buf.at[z, place, :, lanes(j)]
            when(here, lambda: pltpu.make_async_copy(src, dst, sem_dr.at[j]).start())
            to = ((e // 2) * 2 + core, (e % 2) * NX + x)
            when(
                jnp.logical_not(here),
                lambda: remote(src, dst, sem_ds.at[j], sem_dr.at[j], to).start(),
            )

        loop(0, E, one)


    when(home, lambda: down_start(wdn.at[z]))
    when(away, lambda: down_start(wrel))
    dispatch(0)
    dispatch(1)
    w1_start()

    weight = jnp.zeros((E, TOK), F32)
    for k in range(ids.shape[0]):
        weight = weight + jnp.where(ids[k:k + 1, :] == expert, gw_ref[k:k + 1, :], 0.0)
    weights = jnp.where(chosen, weight[:, None, :], 0.0).reshape(E * PAD, TOK)
    high = weights.astype(BF16)
    comb[0] = high
    comb[1] = (weights - high.astype(F32)).astype(BF16)
    acc[...] = jnp.zeros_like(acc)
    out_acc[...] = jnp.zeros_like(out_acc)

    def shards(k):
        return [x] if k == 0 else [(x + k) % NX] if k == FAR else [(x - k + NX) % NX, (x + k) % NX]

    def ring(q, k, j, way):
        shard, to = (((x - k + NX) % NX, right), ((x + k) % NX, left))[way]
        halves = way if k == FAR - 1 else slice(None)
        piece = xs.at[halves, shard, pl.ds(q * RQ, RQ), lanes(j)]
        return remote(piece, piece, sem_xs.at[q, k, j, way], sem_xr.at[q, k, j, way], (me, z * NX + to))

    def hring(q, k, way):
        shard, to = (((x - k + NX) % NX, right), ((x + k) % NX, left))[way]
        piece = hid.at[q, shard, way] if k == FAR - 1 else hid.at[q, shard]
        return remote(piece, piece, sem_hs.at[q, k, way], sem_hr.at[q, k, way], (me, z * NX + to))

    def ring_step(q, k):
        for j in range(2):
            for way in range(2):
                ring(q, k - 1, j, way).wait_recv()
                if k < FAR:
                    ring(q, k, j, way).start()

    def hring_step(q, k):
        for way in range(2):
            hring(q, k - 1, way).wait_recv()
            if k < FAR:
                hring(q, k, way).start()

    def multiply(q, zz, shard):
        rows = pl.ds(q * RQ, RQ)
        acc[q, zz] += nt(w1[zz, :, cols(0, shard)], xs[0, shard, rows]) + nt(w1[zz, :, cols(1, shard)], xs[1, shard, rows])

    def multiply_step(q, zz, k):
        for shard in shards(k):
            multiply(q, zz, shard)

    L = 2 * RQ // 3
    sides = [
        jnp.where(iota((RQ, L), 0) == iota((RQ, L), 1) + (L - side * (RQ - L)), 1.0, 0.0)
        * jnp.where((iota((RQ, L), 1) >= RQ - L) == (side == 1), 1.0, 0.0)
        for side in range(2)
    ]
    sides = [a.astype(BF16) for a in sides]
    spread = iota((RQ, HB * PAD), 0) == (iota((RQ, HB * PAD), 1) >> 4) * CAP + (iota((RQ, HB * PAD), 1) & 15)
    spread = jnp.logical_and(spread, (iota((RQ, HB * PAD), 1) & 15) < CAP)
    spread = jnp.where(spread, 1.0, 0.0).astype(BF16)

    def activate(q):
        for zz in range(2):
            g, u = acc[q, zz, 0:U, :], acc[q, zz, U:2 * U, :]
            h = (g / (1.0 + jnp.exp(-g)) * u).astype(BF16)
            hid[q, x, zz, 0:U, :] = h[:, 0:L]
            hid[q, x, zz, U:U + U // 2, :] = (nn(h[0:U // 2], sides[0]) + nn(h[U // 2:U], sides[1])).astype(BF16)
        for way in range(2):
            hring(q, 0, way).start()

    def project(q, shard):
        for way in range(2):
            low, high = hid[q, shard, way, 0:U, :], hid[q, shard, way, U:U + U // 2, :]
            for f in range(2):
                down_rows = wdn[way, f, units(shard), :]
                out_acc[q, f, 0:L, :] += tn(low, down_rows)
                first, last = tn(high, down_rows[0:U // 2]), tn(high, down_rows[U // 2:U])
                out_acc[q, f, L:RQ, :] += first[0:RQ - L] + last[RQ - L:]

    def give_back(q):
        for f in range(2):
            ret_src[q, f] = tn(spread, out_acc[q, f].astype(BF16)).astype(BF16).reshape(HB, PAD, F)

        def one(t):
            i = 2 * t + q
            for f in range(2):
                here = jnp.logical_and(i == pair, f == z)
                src, dst = ret_src.at[q, f, t], ret_buf.at[work]
                when(here, lambda: pltpu.make_async_copy(src, dst, sem_rr.at[0]).start())
                when(
                    jnp.logical_not(here),
                    lambda: remote(src, dst, sem_rs.at[0], sem_rr.at[0], (2 * i + core, f * NX + x)).start(),
                )

        loop(0, HB, one)

    row, col = iota((ROWS, HALF * PAD), 0), iota((ROWS, HALF * PAD), 1)
    pack = jnp.logical_and(row == (col >> 4) * CAP + (col & 15), (col & 15) < CAP)
    pack = jnp.where(pack, 1.0, 0.0).astype(BF16)

    def arrived(sem, j):
        pltpu.make_async_copy(send_buf.at[:, :, lanes(j)], send_buf.at[:, :, lanes(j)], sem).wait()

    for j in range(2):
        arrived(sem_dr.at[j], j)
        for way in range(2):
            rows = recv_buf[way, :, :, j * J:(j + 1) * J].reshape(HALF * PAD, J)
            xs[way, x, :, j * J:(j + 1) * J] = nn(pack, rows).astype(BF16)
        for way in range(2):
            ring(0, 0, j, way).start()
    for j in range(2):
        for way in range(2):
            ring(1, 0, j, way).start()
    w1_arrived(z)
    multiply_step(0, z, 0)
    for n in range(1, FAR + 1):
        ring_step(0, n)
        if n > LAG:
            ring_step(1, n - LAG)
        multiply_step(0, z, n)
        if n >= LAG:
            multiply_step(1, z, n - LAG)

    w1_arrived(other)

    def pass_w():
        for j in range(2):
            w1_pass(j).start()
        down_arrived(wdn.at[z])
        wd_pass(wdn.at[z], z, sibling).start()

    def cross_w():
        down_arrived(wrel)
        wd_pass(wrel, z, across).start()

    when(home, pass_w)
    when(away, cross_w)
    loop(0, NX, lambda k: multiply(0, other, k))
    activate(0)

    def wd_arrived(zz):
        pltpu.make_async_copy(wdn.at[zz], wdn.at[zz], sem_wfr.at[zz]).wait()

    for m in range(1, LAG + 1):
        ring_step(1, FAR - LAG + m)
        hring_step(0, m)
        multiply_step(1, z, FAR - LAG + m)
    loop(0, NX, lambda k: multiply(1, other, k))
    activate(1)

    def wd_home():
        wd_arrived(other)
        wd_pass(wdn.at[other], other, sibling).start()

    def wd_away():
        wd_arrived(z)
        wd_arrived(other)

    when(home, wd_home)
    when(away, wd_away)

    def project_steps(q, low, high):
        for k in range(low, high + 1):
            for shard in shards(k):
                project(q, shard)

    project(0, x)
    loop(1, LAG + 1, lambda k: [project(0, (x - k + NX) % NX), project(0, (x + k) % NX)])
    for m in range(1, FAR - LAG + 1):
        hring_step(0, LAG + m)
        hring_step(1, m)
        project_steps(0, LAG + m, LAG + m)
    give_back(0)
    project(1, x)
    loop(1, FAR - LAG + 1, lambda k: [project(1, (x - k + NX) % NX), project(1, (x + k) % NX)])
    for m in range(1, LAG + 1):
        hring_step(1, FAR - LAG + m)
        project_steps(1, FAR - LAG + m, FAR - LAG + m)
    give_back(1)

    for j in range(2):
        sent = send_buf.at[0:E - 1, :, lanes(j)]
        pltpu.make_async_copy(sent, sent, sem_ds.at[j]).wait()
    for j in range(2):
        w1_own(j, sibling).wait_send()
        when(home, lambda: w1_pass(j).wait_send())
    wd_pass(wdn.at[z], z, sibling).wait_send()
    when(home, lambda: wd_pass(wdn.at[other], other, sibling).wait_send())
    down_all(wrel, lambda c: c.wait_send())

    for q in range(2):
        for k in range(FAR):
            for way in range(2):
                hring(q, k, way).wait_send()
                for j in range(2):
                    ring(q, k, j, way).wait_send()

    sent = ret_buf.at[0:E - 1]
    pltpu.make_async_copy(sent, sent, sem_rs.at[0]).wait()

    pltpu.make_async_copy(ret_buf, ret_buf, sem_rr.at[0]).wait()
    back = ret_buf[...].reshape(E * PAD, F)
    out_ref[...] = (tn(comb[0], back) + tn(comb[1], back)).astype(BF16)


def solution(mesh):
    E, T = mesh.shape["expert"], mesh.shape["tensor"]
    NX = T // 2

    def local(tokens, expert_ids, gate_weights, w_gate, w_up, w_down):
        tok, F = tokens.shape
        U = w_gate.shape[2]
        HALF = E // 2
        HB = HALF // 2
        ROWS = HALF * CAP
        RQ = ROWS // 2
        vmem = pl.BlockSpec(memory_space=pltpu.VMEM)
        hbm = pl.BlockSpec(memory_space=pl.ANY)
        dma = pltpu.SemaphoreType.DMA
        return pl.pallas_call(
            functools.partial(kernel, E, NX),
            out_shape=jax.ShapeDtypeStruct((tok, F), BF16),
            in_specs=[vmem, vmem, vmem, hbm, hbm, hbm],
            out_specs=vmem,
            scratch_shapes=[
                pltpu.VMEM((E, PAD, F), BF16),
                pltpu.VMEM((2, HALF, PAD, F), BF16),
                pltpu.VMEM((2, NX, ROWS, F), BF16),
                pltpu.VMEM((2, 2 * U, T * F), BF16),
                pltpu.VMEM((2, 2, 2 * U, RQ), F32),
                pltpu.VMEM((2, NX, 2, U + U // 2, 2 * RQ // 3), BF16),
                pltpu.VMEM((2, 2, NX * U, F), BF16),
                pltpu.VMEM((2, NX * U, F), BF16),
                pltpu.VMEM((2, 2, RQ, F), F32),
                pltpu.VMEM((2, 2, HB, PAD, F), BF16),
                pltpu.VMEM((E, PAD, F), BF16),
                pltpu.VMEM((2, E * PAD, tok), BF16),
                dma((2,)),
                dma((2,)),
                dma((2, 2)),
                dma((2, 2)),
                dma((NX, 2)),
                dma((NX, 2)),
                dma((2,)),
                dma((2,)),
                dma((2,)),
                dma((2, NX // 2, 2, 2)),
                dma((2, NX // 2, 2, 2)),
                dma((2, NX // 2, 2)),
                dma((2, NX // 2, 2)),
                dma((1,)),
                dma((1,)),
            ],
            compiler_params=pltpu.CompilerParams(
                collective_id=0, has_side_effects=True, vmem_limit_bytes=60 * 2**20
            ),
        )(
            tokens,
            expert_ids.T,
            gate_weights.T,
            w_gate[0].T,
            w_up[0].T,
            w_down[0],
        )

    placed = (
        P("expert", "tensor"),
        P("expert", None),
        P("expert", None),
        P("expert", None, "tensor"),
        P("expert", None, "tensor"),
        P("expert", "tensor", None),
    )
    return jax.shard_map(
        local, mesh=mesh, in_specs=placed, out_specs=P("expert", "tensor"), check_vma=False
    )
```

```python
import functools

import jax
import jax.numpy as jnp
from jax import lax
from jax.experimental import pallas as pl
from jax.experimental.pallas import tpu as pltpu
from jax.sharding import PartitionSpec as P

MESH = pl.DeviceIdType.MESH
BF16, F32, I32 = jnp.bfloat16, jnp.float32, jnp.int32
CAP = 12
PAD = 16
LAG = 2


def nt(a, b):
    return lax.dot_general(a, b, (((1,), (1,)), ((), ())), preferred_element_type=F32)


def nn(a, b):
    return jnp.dot(a, b, preferred_element_type=F32)


def tn(a, b):
    return lax.dot_general(a, b, (((0,), (0,)), ((), ())), preferred_element_type=F32)


def iota(shape, dim):
    return lax.broadcasted_iota(I32, shape, dim)


def loop(low, high, body):
    def step(k, carry):
        body(k)
        return carry

    lax.fori_loop(low, high, step, 0)


def kernel(
    E, NX,
    tok_ref, ids_ref, gw_ref, wg_ref, wu_ref, wd_ref, out_ref,
    send_buf, recv_buf, xs, w1, acc, hid, wdn, wrel, out_acc, ret_src, ret_buf, comb,
    sem_ds, sem_dr, sem_w1s, sem_w1r, sem_wds, sem_wdr, sem_wfs, sem_wfr, sem_wl,
    sem_xs, sem_xr, sem_hs, sem_hr, sem_rs, sem_rr,
):
    HALF = E // 2
    HB = HALF // 2
    TOK, F = tok_ref.shape
    U = wg_ref.shape[0]
    ROWS = HALF * CAP
    RQ = ROWS // 2
    J = F // 2
    FAR = NX // 2
    me = lax.axis_index("expert")
    s = lax.axis_index("tensor")
    z, x = s // NX, s % NX
    pair, core = me // 2, me % 2
    right, left = (x + 1) % NX, (x + NX - 1) % NX
    other = 1 - z
    work = pair * 2 + z
    home = core == z
    place = (pair % 2) * HB + pair // 2
    across = (me, other * NX + x)
    sibling = (pair * 2 + 1 - core, s)

    def remote(src, dst, send, recv, to):
        return pltpu.make_async_remote_copy(
            src_ref=src, dst_ref=dst, send_sem=send, recv_sem=recv, device_id=to, device_id_type=MESH
        )

    def when(condition, body):
        pl.when(condition)(body)

    away = jnp.logical_not(home)

    barrier = pltpu.get_barrier_semaphore()

    def hello(to):
        pl.semaphore_signal(barrier, inc=1, device_id=to, device_id_type=MESH)

    hello(sibling)
    loop(1, NX, lambda d: hello((me, z * NX + (x + d) % NX)))

    def greet(i):
        for zz in range(2):
            when(
                jnp.logical_not(jnp.logical_and(i == pair, zz == z)),
                lambda: hello((2 * i + core, zz * NX + x)),
            )

    loop(0, HALF, greet)

    ids = ids_ref[...]
    expert = iota((E, TOK), 0)
    member = jnp.zeros((E, TOK), jnp.bool_)
    for k in range(ids.shape[0]):
        member = jnp.logical_or(member, ids[k:k + 1, :] == expert)
    before = (iota((TOK, TOK), 0) < iota((TOK, TOK), 1)).astype(BF16)
    rank = nn(member.astype(F32).astype(BF16), before).astype(I32)
    rank = jnp.where(member, rank, PAD)
    chosen = iota((E, PAD, TOK), 1) == rank[:, None, :]
    select = jnp.where(chosen, 1.0, 0.0).reshape(E * PAD, TOK).astype(BF16)
    send_buf[...] = nn(select, tok_ref[...]).astype(BF16).reshape(E, PAD, F)

    pl.semaphore_wait(barrier, 2 * HALF - 1 + NX)

    def cols(zz, xx):
        return pl.ds(pl.multiple_of(zz * (NX * F) + xx * F, F), F)

    def part(zz, j):
        return w1.at[zz, j * U:(j + 1) * U]

    def w1_own(j, to):
        return remote((wg_ref, wu_ref)[j], part(z, j), sem_w1s.at[0, j], sem_w1r.at[z, j], to)

    def w1_local(j):
        return pltpu.make_async_copy((wg_ref, wu_ref)[j], part(z, j), sem_w1r.at[z, j])

    def w1_pass(j):
        return remote(part(other, j), part(other, j), sem_w1s.at[1, j], sem_w1r.at[other, j], sibling)

    def w1_start():
        for j in range(2):
            when(away, lambda: w1_own(j, across).start())
        for j in range(2):
            when(home, lambda: w1_own(j, sibling).start())
            when(home, lambda: w1_local(j).start())

    def w1_arrived(zz):
        for j in range(2):
            pltpu.make_async_copy(part(zz, j), part(zz, j), sem_w1r.at[zz, j]).wait()

    def units(xx):
        return pl.ds(pl.multiple_of(xx * U, U), U)

    def down(d, f, buf):
        to = (x + d) % NX
        return remote(
            wd_ref.at[:, cols(f, to)], buf.at[f, units(x)], sem_wds.at[d, f], sem_wdr.at[d, f],
            (me, z * NX + to),
        )

    def down_local(f, buf):
        return pltpu.make_async_copy(wd_ref.at[:, cols(f, x)], buf.at[f, units(x)], sem_wl.at[f])

    def down_all(buf, act):
        loop(1, NX, lambda d: [act(down(d, f, buf)) for f in range(2)])

    def down_start(buf):
        for f in range(2):
            down_local(f, buf).start()
        down_all(buf, lambda c: c.start())

    def down_arrived(buf):
        for f in range(2):
            down_local(f, buf).wait()
        down_all(buf, lambda c: c.wait_recv())

    def wd_pass(src, zz, to):
        return remote(src, wdn.at[zz], sem_wfs.at[zz], sem_wfr.at[zz], to)


    def lanes(j):
        return pl.ds(j * J, J)

    def dispatch(j):
        def one(e):
            here = e == work
            src, dst = send_buf.at[e, :, lanes(j)], recv_buf.at[z, place, :, lanes(j)]
            when(here, lambda: pltpu.make_async_copy(src, dst, sem_dr.at[j]).start())
            to = ((e // 2) * 2 + core, (e % 2) * NX + x)
            when(
                jnp.logical_not(here),
                lambda: remote(src, dst, sem_ds.at[j], sem_dr.at[j], to).start(),
            )

        loop(0, E, one)


    when(home, lambda: down_start(wdn.at[z]))
    when(away, lambda: down_start(wrel))
    dispatch(0)
    dispatch(1)
    w1_start()

    weight = jnp.zeros((E, TOK), F32)
    for k in range(ids.shape[0]):
        weight = weight + jnp.where(ids[k:k + 1, :] == expert, gw_ref[k:k + 1, :], 0.0)
    weights = jnp.where(chosen, weight[:, None, :], 0.0).reshape(E * PAD, TOK)
    high = weights.astype(BF16)
    low = (weights - high.astype(F32)).astype(BF16)
    eye = jnp.where(iota((TOK, TOK), 0) == iota((TOK, TOK), 1), 1.0, 0.0).astype(BF16)
    comb[0:TOK, :] = nt(eye, high).astype(BF16)
    comb[TOK:2 * TOK, :] = nt(eye, low).astype(BF16)
    acc[...] = jnp.zeros_like(acc)
    out_acc[...] = jnp.zeros_like(out_acc)

    def shards(k):
        return [x] if k == 0 else [(x + k) % NX] if k == FAR else [(x - k + NX) % NX, (x + k) % NX]

    def ring(q, k, j, way):
        shard, to = (((x - k + NX) % NX, right), ((x + k) % NX, left))[way]
        halves = way if k == FAR - 1 else slice(None)
        piece = xs.at[halves, shard, pl.ds(q * RQ, RQ), lanes(j)]
        return remote(piece, piece, sem_xs.at[q, k, j, way], sem_xr.at[q, k, j, way], (me, z * NX + to))

    def hring(q, k, way):
        shard, to = (((x - k + NX) % NX, right), ((x + k) % NX, left))[way]
        piece = hid.at[q, shard, way] if k == FAR - 1 else hid.at[q, shard]
        return remote(piece, piece, sem_hs.at[q, k, way], sem_hr.at[q, k, way], (me, z * NX + to))

    def ring_step(q, k):
        for j in range(2):
            for way in range(2):
                ring(q, k - 1, j, way).wait_recv()
                if k < FAR:
                    ring(q, k, j, way).start()

    def hring_step(q, k):
        for way in range(2):
            hring(q, k - 1, way).wait_recv()
            if k < FAR:
                hring(q, k, way).start()

    def multiply(q, zz, shard):
        rows = pl.ds(q * RQ, RQ)
        acc[q, zz] += nt(w1[zz, :, cols(0, shard)], xs[0, shard, rows]) + nt(w1[zz, :, cols(1, shard)], xs[1, shard, rows])

    def multiply_step(q, zz, k):
        for shard in shards(k):
            multiply(q, zz, shard)

    L = 2 * RQ // 3
    sides = [
        jnp.where(iota((RQ, L), 0) == iota((RQ, L), 1) + (L - side * (RQ - L)), 1.0, 0.0)
        * jnp.where((iota((RQ, L), 1) >= RQ - L) == (side == 1), 1.0, 0.0)
        for side in range(2)
    ]
    sides = [a.astype(BF16) for a in sides]
    spread = iota((RQ, HB * PAD), 0) == (iota((RQ, HB * PAD), 1) >> 4) * CAP + (iota((RQ, HB * PAD), 1) & 15)
    spread = jnp.logical_and(spread, (iota((RQ, HB * PAD), 1) & 15) < CAP)
    spread = jnp.where(spread, 1.0, 0.0).astype(BF16)

    def activate(q):
        for zz in range(2):
            g, u = acc[q, zz, 0:U, :], acc[q, zz, U:2 * U, :]
            h = (g / (1.0 + jnp.exp(-g)) * u).astype(BF16)
            hid[q, x, zz, 0:U, :] = h[:, 0:L]
            hid[q, x, zz, U:U + U // 2, :] = (nn(h[0:U // 2], sides[0]) + nn(h[U // 2:U], sides[1])).astype(BF16)
        for way in range(2):
            hring(q, 0, way).start()

    def project(q, shard):
        for way in range(2):
            low, high = hid[q, shard, way, 0:U, :], hid[q, shard, way, U:U + U // 2, :]
            for f in range(2):
                down_rows = wdn[way, f, units(shard), :]
                out_acc[q, f, 0:L, :] += tn(low, down_rows)
                first, last = tn(high, down_rows[0:U // 2]), tn(high, down_rows[U // 2:U])
                out_acc[q, f, L:RQ, :] += first[0:RQ - L] + last[RQ - L:]

    def give_back(q):
        for f in range(2):
            ret_src[q, f] = tn(spread, out_acc[q, f].astype(BF16)).astype(BF16).reshape(HB, PAD, F)

        def one(t):
            i = 2 * t + q
            for f in range(2):
                here = jnp.logical_and(i == pair, f == z)
                src, dst = ret_src.at[q, f, t], ret_buf.at[work]
                when(here, lambda: pltpu.make_async_copy(src, dst, sem_rr.at[0]).start())
                when(
                    jnp.logical_not(here),
                    lambda: remote(src, dst, sem_rs.at[0], sem_rr.at[0], (2 * i + core, f * NX + x)).start(),
                )

        loop(0, HB, one)

    row, col = iota((ROWS, HALF * PAD), 0), iota((ROWS, HALF * PAD), 1)
    pack = jnp.logical_and(row == (col >> 4) * CAP + (col & 15), (col & 15) < CAP)
    pack = jnp.where(pack, 1.0, 0.0).astype(BF16)

    def arrived(sem, j):
        pltpu.make_async_copy(send_buf.at[:, :, lanes(j)], send_buf.at[:, :, lanes(j)], sem).wait()

    for j in range(2):
        arrived(sem_dr.at[j], j)
        for way in range(2):
            rows = recv_buf[way, :, :, j * J:(j + 1) * J].reshape(HALF * PAD, J)
            xs[way, x, :, j * J:(j + 1) * J] = nn(pack, rows).astype(BF16)
        for way in range(2):
            ring(0, 0, j, way).start()
    for j in range(2):
        for way in range(2):
            ring(1, 0, j, way).start()
    def pass_w():
        for j in range(2):
            w1_pass(j).start()
        down_arrived(wdn.at[z])
        wd_pass(wdn.at[z], z, sibling).start()

    def cross_w():
        down_arrived(wrel)
        wd_pass(wrel, z, across).start()

    w1_arrived(z)
    multiply_step(0, z, 0)
    for n in range(1, FAR + 1):
        if n == FAR:
            w1_arrived(other)
            when(home, pass_w)
            when(away, cross_w)
            loop(0, NX - 1, lambda k: multiply(0, other, (x + FAR + 1 + k) % NX))
        ring_step(0, n)
        if n > LAG:
            ring_step(1, n - LAG)
        multiply_step(0, z, n)
        if n < FAR and n >= LAG:
            multiply_step(1, z, n - LAG)
    multiply_step(0, other, FAR)
    activate(0)
    multiply_step(1, z, FAR - LAG)

    def wd_arrived(zz):
        pltpu.make_async_copy(wdn.at[zz], wdn.at[zz], sem_wfr.at[zz]).wait()

    for m in range(1, LAG + 1):
        if m == LAG:
            loop(0, NX - 1, lambda k: multiply(1, other, (x + FAR + 1 + k) % NX))
        ring_step(1, FAR - LAG + m)
        hring_step(0, m)
        multiply_step(1, z, FAR - LAG + m)
    multiply_step(1, other, FAR)
    activate(1)

    def wd_home():
        wd_arrived(other)
        wd_pass(wdn.at[other], other, sibling).start()

    def wd_away():
        wd_arrived(z)
        wd_arrived(other)

    when(home, wd_home)
    when(away, wd_away)

    def project_steps(q, low, high):
        for k in range(low, high + 1):
            for shard in shards(k):
                project(q, shard)

    project(0, x)
    loop(1, LAG + 1, lambda k: [project(0, (x - k + NX) % NX), project(0, (x + k) % NX)])
    for m in range(1, FAR - LAG + 1):
        hring_step(0, LAG + m)
        hring_step(1, m)
        project_steps(0, LAG + m, LAG + m)
    give_back(0)
    project(1, x)
    loop(1, FAR - LAG + 1, lambda k: [project(1, (x - k + NX) % NX), project(1, (x + k) % NX)])
    for m in range(1, LAG + 1):
        hring_step(1, FAR - LAG + m)
        project_steps(1, FAR - LAG + m, FAR - LAG + m)
    give_back(1)

    for j in range(2):
        sent = send_buf.at[0:E - 1, :, lanes(j)]
        pltpu.make_async_copy(sent, sent, sem_ds.at[j]).wait()
    for j in range(2):
        w1_own(j, sibling).wait_send()
        when(home, lambda: w1_pass(j).wait_send())
    wd_pass(wdn.at[z], z, sibling).wait_send()
    when(home, lambda: wd_pass(wdn.at[other], other, sibling).wait_send())
    down_all(wrel, lambda c: c.wait_send())

    for q in range(2):
        for k in range(FAR):
            for way in range(2):
                hring(q, k, way).wait_send()
                for j in range(2):
                    ring(q, k, j, way).wait_send()

    sent = ret_buf.at[0:E - 1]
    pltpu.make_async_copy(sent, sent, sem_rs.at[0]).wait()

    pltpu.make_async_copy(ret_buf, ret_buf, sem_rr.at[0]).wait()
    back = ret_buf[...].reshape(E * PAD, F)
    mixed = nn(comb[...], back)
    out_ref[...] = (mixed[0:TOK] + mixed[TOK:2 * TOK]).astype(BF16)


def solution(mesh):
    E, T = mesh.shape["expert"], mesh.shape["tensor"]
    NX = T // 2

    def local(tokens, expert_ids, gate_weights, w_gate, w_up, w_down):
        tok, F = tokens.shape
        U = w_gate.shape[2]
        HALF = E // 2
        HB = HALF // 2
        ROWS = HALF * CAP
        RQ = ROWS // 2
        vmem = pl.BlockSpec(memory_space=pltpu.VMEM)
        hbm = pl.BlockSpec(memory_space=pl.ANY)
        dma = pltpu.SemaphoreType.DMA
        return pl.pallas_call(
            functools.partial(kernel, E, NX),
            out_shape=jax.ShapeDtypeStruct((tok, F), BF16),
            in_specs=[vmem, vmem, vmem, hbm, hbm, hbm],
            out_specs=vmem,
            scratch_shapes=[
                pltpu.VMEM((E, PAD, F), BF16),
                pltpu.VMEM((2, HALF, PAD, F), BF16),
                pltpu.VMEM((2, NX, ROWS, F), BF16),
                pltpu.VMEM((2, 2 * U, T * F), BF16),
                pltpu.VMEM((2, 2, 2 * U, RQ), F32),
                pltpu.VMEM((2, NX, 2, U + U // 2, 2 * RQ // 3), BF16),
                pltpu.VMEM((2, 2, NX * U, F), BF16),
                pltpu.VMEM((2, NX * U, F), BF16),
                pltpu.VMEM((2, 2, RQ, F), F32),
                pltpu.VMEM((2, 2, HB, PAD, F), BF16),
                pltpu.VMEM((E, PAD, F), BF16),
                pltpu.VMEM((2 * tok, E * PAD), BF16),
                dma((2,)),
                dma((2,)),
                dma((2, 2)),
                dma((2, 2)),
                dma((NX, 2)),
                dma((NX, 2)),
                dma((2,)),
                dma((2,)),
                dma((2,)),
                dma((2, NX // 2, 2, 2)),
                dma((2, NX // 2, 2, 2)),
                dma((2, NX // 2, 2)),
                dma((2, NX // 2, 2)),
                dma((1,)),
                dma((1,)),
            ],
            compiler_params=pltpu.CompilerParams(
                collective_id=0, has_side_effects=True, vmem_limit_bytes=60 * 2**20
            ),
        )(
            tokens,
            expert_ids.T,
            gate_weights.T,
            w_gate[0].T,
            w_up[0].T,
            w_down[0],
        )

    placed = (
        P("expert", "tensor"),
        P("expert", None),
        P("expert", None),
        P("expert", None, "tensor"),
        P("expert", None, "tensor"),
        P("expert", "tensor", None),
    )
    return jax.shard_map(
        local, mesh=mesh, in_specs=placed, out_specs=P("expert", "tensor"), check_vma=False
    )
```
